32 devices in a mesh: mol: 2 (over y), row: 16 (over z, x, core).
Axes of the slice: x: 2, y: 2, z: 4, core: 2. Of those that a mesh axis runs over, the one named last changes fastest.
Arguments:
- ia_factor: bfloat16 [768, 3456], P(('mol', 'row')), parts along dimension 0, may hold values from -0.3984375 to 0.3984375
- jb_factor: bfloat16 [221184, 3456], P(('mol', 'row')), parts along dimension 0, may hold values from -0.3984375 to 0.3984375
- eps_occ: float32 [192], P('mol'), parts along dimension 0, may hold values from -2 to -0.3
- eps_vir: float32 [2304], P('mol'), parts along dimension 0, may hold values from 0.2 to 3
Outputs:
- gamma_ia: float32 [768, 3456], P('mol', 'row'), parts along dimension 0
- gamma_jb: bfloat16 [221184, 3456], P(('mol', 'row')), parts along dimension 0
The draws below stay inside these ranges and needn't reach their ends.
There are 2 independent parts, one for each index of `mol`. The reference program is written for one: setup_inputs(seed, part) draws one part's arguments, and reference() takes and returns one part's arrays. A program takes and returns all parts, laid end to end along the dimension named above; each array names one. Nothing has to cross between parts.
All inputs are finite; a program needn't handle non-finite values.
Results may differ from the reference program's by a relative error of at most 0.0047.
Values may be sent and summed in bfloat16 or wider, within the bound.
A program may use at most 256 MiB of HBM per device.

```python
import jax
import jax.numpy as jnp

O = 96
V = 1152
NAUX = 3456
A = 4
IA = 384
JB = 110592


def block_levels(stream_key, shape, split, least, top_value):
    loudness, own = 1.0, jax.random.fold_in(stream_key, 6)
    for position, shards_of in split:
        heights = jnp.exp(jax.random.uniform(jax.random.fold_in(own, position), (shards_of,), jnp.float32, least / len(split), top_value / len(split)))
        loudness = loudness * jnp.repeat(heights, shape[position] // shards_of).reshape([-1 if axis == position else 1 for axis in range(len(shape))])
    return loudness


def bell_draw(key, shape, scale, most, cuts=(), held_as=jnp.bfloat16):
    result = scale * jax.random.normal(key, shape, jnp.float32)
    if cuts:
        result = result * block_levels(key, shape, cuts, -0.22, 0.18)
    return jnp.clip(result, -most, most).astype(held_as)


def setup_inputs(seed: int = 0, part: int = 0) -> dict:
    streams_of = jax.random.split(jax.random.key(seed), 5)
    part_splits = jax.random.split(jax.random.fold_in(streams_of[4], part), 5)
    ia_factor = bell_draw(part_splits[0], (IA, NAUX), 0.05, 0.3984375, ((0, 16),))
    jb_factor = bell_draw(part_splits[1], (JB, NAUX), 0.05, 0.3984375, ((0, 16),))
    eps_occ = jnp.clip(jax.random.uniform(part_splits[2], (O,), jnp.float32, -2.0, -0.3), -2.0, -0.3)
    eps_vir = jnp.clip(jax.random.uniform(part_splits[3], (V,), jnp.float32, 0.2, 3.0), 0.2, 3.0)
    return {"ia_factor": ia_factor, "jb_factor": jb_factor, "eps_occ": eps_occ, "eps_vir": eps_vir}


os_scale = 1.3


def reference(ia_factor, jb_factor, eps_occ, eps_vir):
    coulomb = jnp.dot(ia_factor, jb_factor.T, preferred_element_type=jnp.float32)
    e_ia = (eps_vir[:A][None, :] - eps_occ[:, None]).reshape(-1)
    e_jb = (eps_vir[None, :] - eps_occ[:, None]).reshape(-1)
    amplitude = (-os_scale * coulomb / (e_ia[:, None] + e_jb[None, :])).astype(jnp.bfloat16)
    gamma_ia = jnp.dot(amplitude, jb_factor, preferred_element_type=jnp.float32)
    gamma_jb = jnp.dot(amplitude.T, ia_factor, preferred_element_type=jnp.float32).astype(jnp.bfloat16)
    return gamma_ia, gamma_jb
```

```python
import functools

import jax
import jax.numpy as jnp
from jax import lax
from jax.experimental import pallas as pl
from jax.experimental.pallas import tpu as pltpu
from jax.sharding import PartitionSpec as P

A = 4
os_scale = 1.3
MESH = pl.DeviceIdType.MESH


def bit_orders(n):
    bits = n.bit_length() - 1
    first = [b for b in (1,) if b < bits]
    far = list(range(bits - 1, 1, -1))
    near = [0] if bits else []
    return first + far + near, far + first + near


def subsets(bits):
    out = [0]
    for b in bits:
        out = out + [s | (1 << b) for s in out]
    return out


def flip(me, mask, bits):
    for b in range(bits):
        if mask >> b & 1:
            me = me + (1 << b) * (1 - 2 * ((me // (1 << b)) % 2))
    return me


def enter(me, bits):
    barrier = pltpu.get_barrier_semaphore()
    for b in range(bits):
        pl.semaphore_signal(
            barrier, inc=1, device_id={"row": flip(me, 1 << b, bits)}, device_id_type=MESH
        )
    pl.semaphore_wait(barrier, bits)


def gather_kernel(n, spans, x_ref, out_ref, own_sem, send_sem, recv_sem):
    bits = n.bit_length() - 1
    me = lax.axis_index("row")
    own = pltpu.make_async_copy(x_ref, out_ref.at[me], own_sem)
    own.start()
    enter(me, bits)

    def copy(h, m, b):
        start, size = spans[h]
        s = m ^ (1 << b)
        block = flip(me, s, bits)
        src = x_ref if s == 0 else out_ref.at[block]
        return pltpu.make_async_remote_copy(
            src_ref=src.at[:, pl.ds(start, size)],
            dst_ref=out_ref.at[block, :, pl.ds(start, size)],
            send_sem=send_sem.at[h, m],
            recv_sem=recv_sem.at[h, m],
            device_id={"row": flip(me, 1 << b, bits)},
            device_id_type=MESH,
        )

    orders = bit_orders(n)
    started = {}
    for p in range(bits):
        for h in range(2):
            b = orders[h][p]
            for s in subsets(orders[h][:p]):
                if s:
                    started[h, s].wait_recv()
                m = s | (1 << b)
                started[h, m] = Once(copy(h, m, b))
                started[h, m].start()
    for c in started.values():
        c.wait_recv()
        c.wait_send()
    own.wait()


class Once:
    def __init__(self, copy):
        self.copy, self.got = copy, False

    def start(self):
        self.copy.start()

    def wait_send(self):
        self.copy.wait_send()

    def wait_recv(self):
        if not self.got:
            self.got = True
            self.copy.wait_recv()


def gather(ia, n):
    r, c = ia.shape
    half = (c // 128 + 1) // 2 * 128
    spans = ((0, half), (half, c - half))
    return pl.pallas_call(
        functools.partial(gather_kernel, n, spans),
        out_shape=jax.ShapeDtypeStruct((n, r, c), ia.dtype),
        in_specs=[pl.BlockSpec(memory_space=pl.ANY)],
        out_specs=pl.BlockSpec(memory_space=pl.ANY),
        scratch_shapes=[
            pltpu.SemaphoreType.DMA,
            pltpu.SemaphoreType.DMA((2, n)),
            pltpu.SemaphoreType.DMA((2, n)),
        ],
        compiler_params=pltpu.CompilerParams(collective_id=0, has_side_effects=True),
        name="gather_ia",
    )(ia)


def dense_kernel(n, ia_ref, jb_ref, eia_ref, ejb_ref, gjb_ref, part_ref, acc):
    step = pl.program_id(0)

    @pl.when(step == 0)
    def _():
        acc[...] = jnp.zeros_like(acc)

    coulomb = lax.dot_general(
        ia_ref[...], jb_ref[...], (((1,), (1,)), ((), ())), preferred_element_type=jnp.float32
    )
    denom = eia_ref[...] + ejb_ref[0]
    amp = (-os_scale * coulomb / denom).astype(jnp.bfloat16)
    gjb_ref[...] = lax.dot_general(
        amp, ia_ref[...], (((0,), (0,)), ((), ())), preferred_element_type=jnp.float32
    ).astype(jnp.bfloat16)
    acc[...] += jnp.dot(amp, jb_ref[...], preferred_element_type=jnp.float32)

    @pl.when(step == pl.num_programs(0) - 1)
    def _():
        w = part_ref.shape[2]
        for d in range(n):
            part_ref[d] = acc[:, d * w : (d + 1) * w]


def tile_of(rows):
    for t in (256, 768, 384, 288, 128):
        if rows % t == 0:
            return t
    return rows


def dense(ia, jb, e_ia, e_jb, n):
    m, c = ia.shape
    rows = jb.shape[0]
    t = tile_of(rows)
    return pl.pallas_call(
        functools.partial(dense_kernel, n),
        grid=(rows // t,),
        out_shape=(
            jax.ShapeDtypeStruct((rows, c), jnp.bfloat16),
            jax.ShapeDtypeStruct((n, m, c // n), jnp.float32),
        ),
        in_specs=[
            pl.BlockSpec((m, c), lambda i: (0, 0)),
            pl.BlockSpec((t, c), lambda i: (i, 0)),
            pl.BlockSpec((m, 1), lambda i: (0, 0)),
            pl.BlockSpec((1, 1, t), lambda i: (i, 0, 0)),
        ],
        out_specs=(
            pl.BlockSpec((t, c), lambda i: (i, 0)),
            pl.BlockSpec((n, m, c // n), lambda i: (0, 0, 0)),
        ),
        scratch_shapes=[pltpu.VMEM((m, c), jnp.float32)],
        compiler_params=pltpu.CompilerParams(
            dimension_semantics=("arbitrary",), vmem_limit_bytes=60 * 2**20
        ),
        cost_estimate=pl.CostEstimate(
            flops=6 * m * rows * c, bytes_accessed=4 * rows * c, transcendentals=0
        ),
        name="densities",
    )(ia, jb, e_ia, e_jb.reshape(rows // t, 1, t))


def reduce_kernel(n, part_hbm, out_ref, part_ref, stage, recv, load_sem, send_sem, recv_sem):
    bits = n.bit_length() - 1
    me = lax.axis_index("row")
    half = part_ref.shape[1] // 2
    load = pltpu.make_async_copy(part_hbm, part_ref, load_sem)
    load.start()
    enter(me, bits)
    load.wait()
    orders = [order[::-1] for order in bit_orders(n)]
    copies = []
    pending = {}
    for p in range(bits):
        for h in range(2):
            rows = pl.ds(h * half, half)
            if p:
                for s, m in pending[h]:
                    keep = flip(me, s, bits)
                    part_ref[keep, rows] = part_ref[keep, rows] + recv[h, m].astype(jnp.float32)
            b = orders[h][p]
            sent = []
            for s in subsets(orders[h][p + 1 :]):
                m = s | (1 << b)
                stage[h, m] = part_ref[flip(me, m, bits), rows].astype(jnp.bfloat16)
                c = pltpu.make_async_remote_copy(
                    src_ref=stage.at[h, m],
                    dst_ref=recv.at[h, m],
                    send_sem=send_sem.at[h, m],
                    recv_sem=recv_sem.at[h, m],
                    device_id={"row": flip(me, 1 << b, bits)},
                    device_id_type=MESH,
                )
                c.start()
                copies.append(c)
                sent.append((s, m, c))
            pending[h] = [Pair(s, m, c) for s, m, c in sent]
    for h in range(2):
        rows = pl.ds(h * half, half)
        for s, m in pending[h]:
            out_ref[rows] = part_ref[me, rows] + recv[h, m].astype(jnp.float32)
    for c in copies:
        c.wait_send()


class Pair:
    def __init__(self, s, m, copy):
        self.s, self.m, self.copy = s, m, copy

    def __iter__(self):
        self.copy.wait_recv()
        return iter((self.s, self.m))


def reduce_scatter(part, n):
    _, m, w = part.shape
    return pl.pallas_call(
        functools.partial(reduce_kernel, n),
        out_shape=jax.ShapeDtypeStruct((m, w), jnp.float32),
        in_specs=[pl.BlockSpec(memory_space=pl.ANY)],
        out_specs=pl.BlockSpec(memory_space=pltpu.VMEM),
        scratch_shapes=[
            pltpu.VMEM((n, m, w), jnp.float32),
            pltpu.VMEM((2, n, m // 2, w), jnp.bfloat16),
            pltpu.VMEM((2, n, m // 2, w), jnp.bfloat16),
            pltpu.SemaphoreType.DMA,
            pltpu.SemaphoreType.DMA((2, n)),
            pltpu.SemaphoreType.DMA((2, n)),
        ],
        compiler_params=pltpu.CompilerParams(
            collective_id=1, has_side_effects=True, vmem_limit_bytes=60 * 2**20
        ),
        name="reduce_gamma",
    )(part)


def shards(n, ia_factor, jb_factor, eps_occ, eps_vir):
    jb_count = jb_factor.shape[0]
    pairs = (eps_vir[None, :] - eps_occ[:, None]).reshape(-1)
    e_jb = lax.dynamic_slice_in_dim(pairs, lax.axis_index("row") * jb_count, jb_count)
    e_ia = (eps_vir[:A][None, :] - eps_occ[:, None]).reshape(-1, 1)
    all_rows = gather(ia_factor, n).reshape(-1, ia_factor.shape[1])
    gamma_jb, part = dense(all_rows, jb_factor, e_ia, e_jb, n)
    return (reduce_scatter(part, n), gamma_jb)


def solution(mesh):
    placed = (P(("mol", "row"), None), P(("mol", "row"), None), P("mol"), P("mol"))
    return jax.shard_map(
        functools.partial(shards, mesh.shape["row"]),
        mesh=mesh,
        in_specs=placed,
        out_specs=(P("mol", "row"), P(("mol", "row"), None)),
        check_vma=False,
    )
```

```python
import functools

import jax
import jax.numpy as jnp
from jax import lax
from jax.experimental import pallas as pl
from jax.experimental.pallas import tpu as pltpu
from jax.sharding import PartitionSpec as P

A = 4
os_scale = 1.3
MESH = pl.DeviceIdType.MESH


def bit_orders(n):
    bits = n.bit_length() - 1
    first = [b for b in (1,) if b < bits]
    far = list(range(bits - 1, 1, -1))
    near = [0] if bits else []
    return first + far + near, far + first + near


def subsets(bits):
    out = [0]
    for b in bits:
        out = out + [s | (1 << b) for s in out]
    return out


def flip(me, mask, bits):
    for b in range(bits):
        if mask >> b & 1:
            me = me + (1 << b) * (1 - 2 * ((me // (1 << b)) % 2))
    return me


def enter(me, bits):
    barrier = pltpu.get_barrier_semaphore()
    for b in range(bits):
        pl.semaphore_signal(
            barrier, inc=1, device_id={"row": flip(me, 1 << b, bits)}, device_id_type=MESH
        )
    pl.semaphore_wait(barrier, bits)


def gather_kernel(n, spans, x_ref, out_ref, own_sem, send_sem, recv_sem):
    bits = n.bit_length() - 1
    me = lax.axis_index("row")
    own = pltpu.make_async_copy(x_ref, out_ref.at[me], own_sem)
    own.start()
    enter(me, bits)

    def copy(h, m, b):
        start, size = spans[h]
        s = m ^ (1 << b)
        block = flip(me, s, bits)
        src = x_ref if s == 0 else out_ref.at[block]
        return pltpu.make_async_remote_copy(
            src_ref=src.at[:, pl.ds(start, size)],
            dst_ref=out_ref.at[block, :, pl.ds(start, size)],
            send_sem=send_sem.at[h, m],
            recv_sem=recv_sem.at[h, m],
            device_id={"row": flip(me, 1 << b, bits)},
            device_id_type=MESH,
        )

    orders = bit_orders(n)
    started = {}
    for p in range(bits):
        for h in range(2):
            b = orders[h][p]
            for s in subsets(orders[h][:p]):
                if s:
                    started[h, s].wait_recv()
                m = s | (1 << b)
                started[h, m] = Once(copy(h, m, b))
                started[h, m].start()
    for c in started.values():
        c.wait_recv()
        c.wait_send()
    own.wait()


class Once:
    def __init__(self, copy):
        self.copy, self.got = copy, False

    def start(self):
        self.copy.start()

    def wait_send(self):
        self.copy.wait_send()

    def wait_recv(self):
        if not self.got:
            self.got = True
            self.copy.wait_recv()


def gather(ia, n):
    r, c = ia.shape
    half = (c // 128 + 1) // 2 * 128
    spans = ((0, half), (half, c - half))
    return pl.pallas_call(
        functools.partial(gather_kernel, n, spans),
        out_shape=jax.ShapeDtypeStruct((n, r, c), ia.dtype),
        in_specs=[pl.BlockSpec(memory_space=pl.ANY)],
        out_specs=pl.BlockSpec(memory_space=pl.ANY),
        scratch_shapes=[
            pltpu.SemaphoreType.DMA,
            pltpu.SemaphoreType.DMA((2, n)),
            pltpu.SemaphoreType.DMA((2, n)),
        ],
        compiler_params=pltpu.CompilerParams(collective_id=0, has_side_effects=True),
        name="gather_ia",
    )(ia)


def dense_kernel(n, ia_ref, jb_ref, eia_ref, ejb_ref, gjb_ref, part_ref, acc):
    step = pl.program_id(0)

    @pl.when(step == 0)
    def _():
        acc[...] = jnp.zeros_like(acc)

    coulomb = lax.dot_general(
        jb_ref[...], ia_ref[...], (((1,), (1,)), ((), ())), preferred_element_type=jnp.float32
    )
    e_jb = jnp.broadcast_to(ejb_ref[0], (128, ejb_ref.shape[2])).T
    denom = eia_ref[...] + e_jb[:, :1]
    amp = (-os_scale * coulomb / denom).astype(jnp.bfloat16)
    gjb_ref[...] = jnp.dot(
        amp, ia_ref[...], preferred_element_type=jnp.float32
    ).astype(jnp.bfloat16)
    acc[...] += jnp.dot(amp.T, jb_ref[...], preferred_element_type=jnp.float32)

    @pl.when(step == pl.num_programs(0) - 1)
    def _():
        w = part_ref.shape[2]
        for d in range(n):
            part_ref[d] = acc[:, d * w : (d + 1) * w]


def tile_of(rows):
    for t in (768, 256, 384, 288, 128):
        if rows % t == 0:
            return t
    return rows


def dense(ia, jb, e_ia, e_jb, n):
    m, c = ia.shape
    rows = jb.shape[0]
    t = tile_of(rows)
    return pl.pallas_call(
        functools.partial(dense_kernel, n),
        grid=(rows // t,),
        out_shape=(
            jax.ShapeDtypeStruct((rows, c), jnp.bfloat16),
            jax.ShapeDtypeStruct((n, m, c // n), jnp.float32),
        ),
        in_specs=[
            pl.BlockSpec((m, c), lambda i: (0, 0), pipeline_mode=pl.Buffered(1)),
            pl.BlockSpec((t, c), lambda i: (i, 0)),
            pl.BlockSpec((1, m), lambda i: (0, 0)),
            pl.BlockSpec((1, 1, t), lambda i: (i, 0, 0)),
        ],
        out_specs=(
            pl.BlockSpec((t, c), lambda i: (i, 0)),
            pl.BlockSpec((n, m, c // n), lambda i: (0, 0, 0), pipeline_mode=pl.Buffered(1)),
        ),
        scratch_shapes=[pltpu.VMEM((m, c), jnp.float32)],
        compiler_params=pltpu.CompilerParams(
            dimension_semantics=("arbitrary",), vmem_limit_bytes=60 * 2**20
        ),
        cost_estimate=pl.CostEstimate(
            flops=6 * m * rows * c, bytes_accessed=4 * rows * c, transcendentals=0
        ),
        name="densities",
    )(ia, jb, e_ia, e_jb.reshape(rows // t, 1, t))


def reduce_kernel(n, part_hbm, out_ref, part_ref, stage, recv, load_sem, send_sem, recv_sem):
    bits = n.bit_length() - 1
    me = lax.axis_index("row")
    half = part_ref.shape[1] // 2
    load = pltpu.make_async_copy(part_hbm, part_ref, load_sem)
    load.start()
    enter(me, bits)
    load.wait()
    orders = [order[::-1] for order in bit_orders(n)]
    copies = []
    pending = {}
    for p in range(bits):
        for h in range(2):
            rows = pl.ds(h * half, half)
            if p:
                for s, m in pending[h]:
                    keep = flip(me, s, bits)
                    part_ref[keep, rows] = part_ref[keep, rows] + recv[h, m].astype(jnp.float32)
            b = orders[h][p]
            sent = []
            for s in subsets(orders[h][p + 1 :]):
                m = s | (1 << b)
                stage[h, m] = part_ref[flip(me, m, bits), rows].astype(jnp.bfloat16)
                c = pltpu.make_async_remote_copy(
                    src_ref=stage.at[h, m],
                    dst_ref=recv.at[h, m],
                    send_sem=send_sem.at[h, m],
                    recv_sem=recv_sem.at[h, m],
                    device_id={"row": flip(me, 1 << b, bits)},
                    device_id_type=MESH,
                )
                c.start()
                copies.append(c)
                sent.append((s, m, c))
            pending[h] = [Pair(s, m, c) for s, m, c in sent]
    for h in range(2):
        rows = pl.ds(h * half, half)
        for s, m in pending[h]:
            out_ref[rows] = part_ref[me, rows] + recv[h, m].astype(jnp.float32)
    for c in copies:
        c.wait_send()


class Pair:
    def __init__(self, s, m, copy):
        self.s, self.m, self.copy = s, m, copy

    def __iter__(self):
        self.copy.wait_recv()
        return iter((self.s, self.m))


def reduce_scatter(part, n):
    _, m, w = part.shape
    return pl.pallas_call(
        functools.partial(reduce_kernel, n),
        out_shape=jax.ShapeDtypeStruct((m, w), jnp.float32),
        in_specs=[pl.BlockSpec(memory_space=pl.ANY)],
        out_specs=pl.BlockSpec(memory_space=pltpu.VMEM),
        scratch_shapes=[
            pltpu.VMEM((n, m, w), jnp.float32),
            pltpu.VMEM((2, n, m // 2, w), jnp.bfloat16),
            pltpu.VMEM((2, n, m // 2, w), jnp.bfloat16),
            pltpu.SemaphoreType.DMA,
            pltpu.SemaphoreType.DMA((2, n)),
            pltpu.SemaphoreType.DMA((2, n)),
        ],
        compiler_params=pltpu.CompilerParams(
            collective_id=1, has_side_effects=True, vmem_limit_bytes=60 * 2**20
        ),
        name="reduce_gamma",
    )(part)


def shards(n, ia_factor, jb_factor, eps_occ, eps_vir):
    jb_count = jb_factor.shape[0]
    pairs = (eps_vir[None, :] - eps_occ[:, None]).reshape(-1)
    e_jb = lax.dynamic_slice_in_dim(pairs, lax.axis_index("row") * jb_count, jb_count)
    e_ia = (eps_vir[:A][None, :] - eps_occ[:, None]).reshape(1, -1)
    all_rows = gather(ia_factor, n).reshape(-1, ia_factor.shape[1])
    gamma_jb, part = dense(all_rows, jb_factor, e_ia, e_jb, n)
    return (reduce_scatter(part, n), gamma_jb)


def solution(mesh):
    placed = (P(("mol", "row"), None), P(("mol", "row"), None), P("mol"), P("mol"))
    return jax.shard_map(
        functools.partial(shards, mesh.shape["row"]),
        mesh=mesh,
        in_specs=placed,
        out_specs=(P("mol", "row"), P(("mol", "row"), None)),
        check_vma=False,
    )
```
